1024 devices in a mesh: expert: 64 (over z, x), cuts: 2 (over core), dp: 8 (over y).
Axes of the slice: x: 4, y: 8, z: 16, core: 2. Of those that a mesh axis runs over, the one named last changes fastest.
Arguments:
- tokens: bfloat16 [12288, 2048], P(('expert', 'dp')), may hold values from -6 to 6
- out_grad: bfloat16 [12288, 2048], P(('expert', 'dp')), may hold values from -6 to 6
- expert_ids: int32 [12288, 8], P(('expert', 'dp')), may hold values from 0 to 63, all different within a row; in each aligned block of 24 rows (0 to 23, 24 to 47, ...) at most 4 rows name the same one
- route_probs: float32 [12288, 8], P(('expert', 'dp')), may hold values from 0.05 to 0.6
- gate_weight: bfloat16 [2048, 64, 768], P(None, 'expert', 'cuts'), may hold values from -0.125 to 0.125
- up_weight: bfloat16 [2048, 64, 768], P(None, 'expert', 'cuts'), may hold values from -0.125 to 0.125
- down_weight: bfloat16 [768, 64, 2048], P('cuts', 'expert'), may hold values from -0.21875 to 0.21875
Outputs:
- token_grad: bfloat16 [12288, 2048], P(('expert', 'dp'), 'cuts')
- gate_grad: bfloat16 [2048, 64, 768], P('dp', 'expert', 'cuts')
- up_grad: bfloat16 [2048, 64, 768], P('dp', 'expert', 'cuts')
- down_grad: bfloat16 [768, 64, 2048], P(('cuts', 'dp'), 'expert')
The draws below stay inside these ranges and needn't reach their ends.
Inputs may be any that keep to these rules, and one draw needn't show every extreme that they name: `expert_ids`: each row names 8 different experts. In each aligned block of 24 rows (the tokens of one device) no expert is named by more than 4 rows, a bound that some block reaches.
All inputs are finite; a program needn't handle non-finite values.
Results may differ from the reference program's by a relative error of at most 0.017.
Values may be sent and summed in bfloat16 or wider, within the bound.
No kernel may reach another device: no remote copies, remote signals or barrier semaphores. Data moves between devices by JAX's collectives and lax.ppermute only.
A program may use at most 64 MiB of HBM per device.

```python
import math
import jax
import jax.numpy as jnp
import numpy as np
from jax import lax

D = 2048
FF = 768
EXPERTS = 64
TOPK = 8
TOK_DEV = 24
CAP = 4
TOKENS = 12288
N_EXPERT = 64
N_DP = 8


def shard_levels(rng, shape, split, low, largest):
    def one(position, shards_of):
        steps = jax.random.uniform(jax.random.fold_in(jax.random.fold_in(rng, 6), position), (shards_of,), jnp.float32, low / len(split), largest / len(split))
        return jnp.repeat(jnp.exp(steps), shape[position] // shards_of).reshape((-1,) + (1,) * (len(shape) - position - 1))

    gain = one(*split[0])
    for cut in split[1:]:
        gain = gain * one(*cut)
    return gain


def shared_out(own_key, own, number, rows, amount, top, reach, skew):
    ranking = jax.random.permutation(own_key, amount)
    crowded, usual = portions_of(amount, rows * top, reach, skew, True), portions_of(amount, rows * top, reach, skew, False)
    places = jnp.arange(amount)

    def named(lengths, offset_by):
        used = int((lengths > 0).sum())
        fixed = max(1, used // 4)
        shifted = fixed + (places - fixed + offset_by * (used - fixed)) % max(1, amount - fixed)
        return jnp.zeros((amount,), jnp.int32).at[ranking[jnp.where(places < fixed, places, shifted)]].set(jnp.asarray(lengths, jnp.int32))

    lengths = jnp.where(number % 4 == 0, named(crowded, number // 4), named(usual, number - number // 4 - 1))
    mixed = jax.random.permutation(jax.random.fold_in(own, 3), amount)
    donor, sink = mixed[0:amount // 2 * 2:2], mixed[1:amount // 2 * 2:2]
    slack = jnp.minimum(lengths[donor] - 1, reach - lengths[sink]) // 2
    slack = jnp.where((donor == ranking[0]) | (sink == ranking[0]) | (lengths[sink] == 0), 0, jnp.maximum(slack, 0))
    shifted = jax.random.randint(jax.random.fold_in(own, 4), (amount // 2,), 0, 1 << 20) % (slack + 1)
    lengths = lengths.at[donor].add(-shifted).at[sink].add(shifted)
    items = jnp.searchsorted(jnp.cumsum(lengths), jnp.arange(rows * top), side="right").astype(jnp.int32)
    listing = items.reshape(top, rows).T
    listing = listing[jax.random.permutation(jax.random.fold_in(own, 1), rows)]
    offset_by = jax.random.randint(jax.random.fold_in(own, 2), (rows, 1), 0, top)
    return jnp.take_along_axis(listing, (jnp.arange(top)[None, :] + offset_by) % top, axis=1)


def portions_of(number_of, total, limit, skew, full):
    portions = [(1 << 20) // math.isqrt(grade ** skew) + 1 for grade in range(1, number_of + 1)]
    largest = limit if full else min(limit, max(-(-total // number_of), total * portions[0] // sum(portions)))
    least = 1 if total - largest >= number_of - 1 else 0
    given, surplus = [largest] + [least] * (number_of - 1), total - largest - least * (number_of - 1)
    while surplus > 0:
        free = [i for i in range(1, number_of) if given[i] < largest] or [i for i in range(1, number_of) if given[i] < limit]
        pool, budget = sum([portions[i] for i in free]), surplus
        for i in free:
            addition = min(limit - given[i], max(1, budget * portions[i] // pool), surplus)
            given[i] = given[i] + addition
            surplus = surplus - addition
    return np.array(given)


def scatter_about(rng, extent, spread, reach, split=(), kind=jnp.bfloat16):
    result = jax.random.normal(rng, extent, jnp.float32) * spread
    if len(split) > 0:
        result = shard_levels(rng, extent, split, -0.22, 0.18) * result
    return jnp.clip(result, min=-reach, max=reach).astype(kind)


def setup_inputs(seed: int = 0) -> dict:
    key_of = jax.random.split(jax.random.key(seed), 8)
    tokens = scatter_about(key_of[0], (TOKENS, D), 1.0, 6.0, ((0, 512),))
    out_grad = scatter_about(key_of[1], (TOKENS, D), 1.0, 6.0, ((0, 512),))
    expert_ids_keys = jax.random.split(jax.random.fold_in(key_of[2], 1), TOKENS // TOK_DEV)
    expert_ids_turns = jax.random.permutation(jax.random.fold_in(key_of[2], 3), TOKENS // TOK_DEV)
    expert_ids = jax.vmap(lambda own, number: shared_out(jax.random.fold_in(key_of[2], 2), own, number, TOK_DEV, EXPERTS, TOPK, CAP, 2))(expert_ids_keys, expert_ids_turns).reshape((TOKENS, TOPK))
    route_probs = jnp.clip(jnp.exp(math.log(0.6) - 2.4849067 * jax.random.uniform(key_of[3], (TOKENS, TOPK), jnp.float32) ** shard_levels(key_of[3], (TOKENS, TOPK), ((0, 512),), -0.2, 0.2)), 0.05, 0.6)
    gate_weight = scatter_about(key_of[4], (D, EXPERTS, FF), D ** -0.5, 0.125, ((1, 64), (2, 2)))
    up_weight = scatter_about(key_of[5], (D, EXPERTS, FF), D ** -0.5, 0.125, ((1, 64), (2, 2)))
    down_weight = scatter_about(key_of[6], (FF, EXPERTS, D), FF ** -0.5, 0.21875, ((0, 2), (1, 64)))
    return {"tokens": tokens, "out_grad": out_grad, "expert_ids": expert_ids, "route_probs": route_probs, "gate_weight": gate_weight, "up_weight": up_weight, "down_weight": down_weight}


def silu_parts(gate_val):
    sigma = jax.nn.sigmoid(gate_val)
    return gate_val * sigma, sigma * (1.0 + gate_val * (1.0 - sigma))


def replica_rows(values):
    last = values.shape[-1]
    grouped = values.reshape(N_EXPERT, N_DP, CAP, last).transpose(1, 0, 2, 3)
    return grouped.reshape(N_DP, N_EXPERT * CAP, last).astype(jnp.float32)


def replica_sum(terms):
    rounded = lax.optimization_barrier(terms.astype(jnp.bfloat16))
    return jnp.sum(rounded.astype(jnp.float32), axis=0).astype(jnp.bfloat16)


def reference(tokens, out_grad, expert_ids, route_probs, gate_weight, up_weight, down_weight):
    blocks = TOKENS // TOK_DEV
    per_block = TOK_DEV * TOPK
    slots = EXPERTS * CAP
    routing = expert_ids.reshape(blocks, per_block)
    onehot = (routing[:, :, None] == jnp.arange(EXPERTS, dtype=jnp.int32)[None, None, :]).astype(jnp.int32)
    earlier = jnp.cumsum(onehot, axis=1) - onehot
    slot_of = (routing * CAP + jnp.sum(earlier * onehot, axis=2)).astype(jnp.int32)
    block_ids = jnp.arange(blocks, dtype=jnp.int32)[:, None]
    assigned = jnp.broadcast_to(jnp.arange(per_block, dtype=jnp.int32)[None, :], (blocks, per_block))
    table = jnp.full((blocks, slots), -1, jnp.int32).at[block_ids, slot_of].set(assigned)
    flat_probs = route_probs.reshape(-1)

    def one_expert(carry, expert_no):
        chosen = lax.dynamic_slice_in_dim(table, (expert_no * CAP).astype(jnp.int32), CAP, 1)
        keep = (chosen >= 0).reshape(-1)
        within = jnp.maximum(chosen, 0)
        token_at = (block_ids * TOK_DEV + within // TOPK).reshape(-1).astype(jnp.int32)
        assign_at = (block_ids * per_block + within).reshape(-1).astype(jnp.int32)
        rows_in = jnp.where(keep[:, None], tokens[token_at], jnp.zeros((), jnp.bfloat16))
        weight_row = jnp.where(keep, flat_probs[assign_at], jnp.zeros((), jnp.float32))
        rows_grad = (weight_row[:, None] * out_grad[token_at].astype(jnp.float32)).astype(jnp.bfloat16)
        w_gate = lax.dynamic_index_in_dim(gate_weight, expert_no, 1, keepdims=False)
        w_upper = lax.dynamic_index_in_dim(up_weight, expert_no, 1, keepdims=False)
        w_down = lax.dynamic_index_in_dim(down_weight, expert_no, 1, keepdims=False)
        gate_val = jnp.dot(rows_in, w_gate, preferred_element_type=jnp.float32)
        up_val = jnp.dot(rows_in, w_upper, preferred_element_type=jnp.float32)
        activated, slope = silu_parts(gate_val)
        hidden = (activated * up_val).astype(jnp.bfloat16)
        back_hid = jnp.dot(rows_grad, w_down.T, preferred_element_type=jnp.float32)
        gate_back = (back_hid * up_val * slope).astype(jnp.bfloat16)
        up_back = (back_hid * activated).astype(jnp.bfloat16)
        row_grads = jnp.dot(gate_back, w_gate.T, preferred_element_type=jnp.float32)
        row_grads = row_grads + jnp.dot(up_back, w_upper.T, preferred_element_type=jnp.float32)
        carry = carry.at[token_at].add(row_grads)
        rows_rep = replica_rows(rows_in)
        gate_sum = replica_sum(jnp.einsum("nrd,nrf->ndf", rows_rep, replica_rows(gate_back)))
        up_sum = replica_sum(jnp.einsum("nrd,nrf->ndf", rows_rep, replica_rows(up_back)))
        down_sum = replica_sum(jnp.einsum("nrf,nrd->nfd", replica_rows(hidden), replica_rows(rows_grad)))
        return carry, (gate_sum, up_sum, down_sum)

    start_grad = jnp.zeros((TOKENS, D), jnp.float32)
    total, stacked = lax.scan(one_expert, start_grad, jnp.arange(EXPERTS, dtype=jnp.int32))
    gates, uppers, downs = stacked
    return (total.astype(jnp.bfloat16), jnp.transpose(gates, (1, 0, 2)),
            jnp.transpose(uppers, (1, 0, 2)), jnp.transpose(downs, (1, 0, 2)))
```

```python
import jax
import jax.numpy as jnp
from jax import lax
from jax.sharding import PartitionSpec as P

EXPERTS = 64
CAP = 4


def shards(tokens, out_grad, expert_ids, route_probs, gate_weight, up_weight, down_weight):
    rows, width = tokens.shape
    top = expert_ids.shape[1]
    half = width // 2
    hidden_dim = gate_weight.shape[2]
    slots = EXPERTS * CAP
    replicas = lax.axis_size("dp")
    cut = lax.axis_index("cuts")
    first = cut == 0
    swap = [(0, 1), (1, 0)]

    named = (
        expert_ids[:, :, None] == jnp.arange(EXPERTS, dtype=jnp.int32)[None, None, :]
    )
    names = jnp.sum(named.astype(jnp.float32), axis=1)
    before = jnp.arange(rows)[:, None] > jnp.arange(rows)[None, :]
    rank = jnp.dot(
        before.astype(jnp.bfloat16), names.astype(jnp.bfloat16), preferred_element_type=jnp.float32
    )
    prob = jnp.sum(jnp.where(named, route_probs[:, :, None], 0.0), axis=1)
    place = jnp.where(names > 0, rank, -1.0)
    slot_rank = jnp.arange(slots) % CAP
    place_t = jnp.repeat(place.T, CAP, axis=0)
    prob_t = jnp.repeat(prob.T, CAP, axis=0)
    hit = place_t == slot_rank[:, None].astype(jnp.float32)
    picked = jnp.where(hit, 1.0, 0.0).astype(jnp.bfloat16)
    weighed = jnp.where(hit, prob_t, 0.0)
    factor = jnp.where(first, picked.astype(jnp.float32), weighed)
    high = lax.reduce_precision(factor, 8, 7)
    middle = lax.reduce_precision(factor - high, 8, 7)
    low = factor - high - middle
    factors = jnp.concatenate((high, middle, low), axis=1).astype(jnp.bfloat16)
    source = jnp.where(first, tokens, out_grad)
    sent = jnp.dot(
        factors, jnp.concatenate((source,) * 3, axis=0), preferred_element_type=jnp.float32
    ).astype(jnp.bfloat16)
    own = lax.all_to_all(
        sent.reshape(EXPERTS, CAP, width), "expert", split_axis=0, concat_axis=0, tiled=True
    ).reshape(slots, width)
    peer = lax.ppermute(own, "cuts", swap)
    rows_in = jnp.where(first, own, peer)
    rows_grad = jnp.where(first, peer, own)

    w_gate = gate_weight[:, 0, :]
    w_up = up_weight[:, 0, :]
    w_down = down_weight[:, 0, :]

    def dot(a, b, da, db):
        return lax.dot_general(a, b, (((da,), (db,)), ((), ())), preferred_element_type=jnp.float32)

    gate_val = dot(rows_in, w_gate, 1, 0)
    up_val = dot(rows_in, w_up, 1, 0)
    sigma = jax.nn.sigmoid(gate_val)
    activated = gate_val * sigma
    slope = sigma * (1.0 + gate_val * (1.0 - sigma))
    hidden = (activated * up_val).astype(jnp.bfloat16)
    back_hid = dot(rows_grad, w_down, 1, 1)
    gate_back = (back_hid * up_val * slope).astype(jnp.bfloat16)
    up_back = (back_hid * activated).astype(jnp.bfloat16)

    tiles = hidden_dim // 128
    share = width // replicas
    strip = hidden_dim // replicas

    def packed(grad):
        return grad.reshape(replicas, share, tiles, 128).transpose(0, 2, 1, 3)

    down = dot(hidden, rows_grad, 0, 0).astype(jnp.bfloat16)
    down = down.reshape(replicas, strip, width // 128, 128).transpose(0, 2, 1, 3)
    parts = [
        packed(dot(rows_in, gate_back, 0, 0).astype(jnp.bfloat16)),
        packed(dot(rows_in, up_back, 0, 0).astype(jnp.bfloat16)),
        down,
    ]
    flat = jnp.concatenate([part.reshape(replicas, tiles * share, 128) for part in parts], axis=1)
    total = lax.psum_scatter(flat, "dp", scatter_dimension=0, tiled=True)[0]

    row_grads = dot(gate_back, w_gate, 1, 1) + dot(up_back, w_up, 1, 1)
    mine = jnp.where(first, row_grads[:, :half], row_grads[:, half:])
    other = jnp.where(first, row_grads[:, half:], row_grads[:, :half])
    mine = mine + lax.ppermute(other.astype(jnp.bfloat16), "cuts", swap).astype(jnp.float32)
    returned = lax.all_to_all(
        mine.astype(jnp.bfloat16).reshape(EXPERTS, CAP, half),
        "expert", split_axis=0, concat_axis=0, tiled=True,
    ).reshape(slots, half)
    result = dot(picked, returned, 0, 0).astype(jnp.bfloat16)

    size = tiles * share

    def unpacked(block):
        return block.reshape(tiles, share, 128).transpose(1, 0, 2).reshape(share, 1, hidden_dim)

    down_grad = (
        total[2 * size :].reshape(width // 128, strip, 128).transpose(1, 0, 2)
        .reshape(strip, 1, width)
    )
    return (result, unpacked(total[:size]), unpacked(total[size : 2 * size]), down_grad)


def solution(mesh):
    placed = (
        P(("expert", "dp"), None),
        P(("expert", "dp"), None),
        P(("expert", "dp"), None),
        P(("expert", "dp"), None),
        P(None, "expert", "cuts"),
        P(None, "expert", "cuts"),
        P("cuts", "expert", None),
    )
    return jax.shard_map(
        shards,
        mesh=mesh,
        in_specs=placed,
        out_specs=(
            P(("expert", "dp"), "cuts"),
            P("dp", "expert", "cuts"),
            P("dp", "expert", "cuts"),
            P(("cuts", "dp"), "expert", None),
        ),
        check_vma=False,
    )
```

```python
import functools

import jax
import jax.numpy as jnp
from jax import lax
from jax.experimental import pallas as pl
from jax.experimental.pallas import tpu as pltpu
from jax.sharding import PartitionSpec as P

EXPERTS = 64
CAP = 4
SLOTS = EXPERTS * CAP
VMEM = pl.BlockSpec(memory_space=pltpu.VMEM)
SMEM = pl.BlockSpec(memory_space=pltpu.SMEM)
ANY = pl.BlockSpec(memory_space=pl.ANY)
PARAMS = pltpu.CompilerParams(vmem_limit_bytes=32 * 1024 * 1024)


def dot(a, b, da, db, precision=None):
    return lax.dot_general(
        a, b, (((da,), (db,)), ((), ())), precision=precision, preferred_element_type=jnp.float32
    )


def send_kernel(cut, ids, probs, tokens, grads, sent, picked):
    rows, top = ids.shape
    lane = lax.broadcasted_iota(jnp.int32, (rows, SLOTS), 1)
    expert = lax.shift_right_logical(lane, 2)
    names = jnp.zeros((rows, SLOTS), jnp.float32)
    weight = jnp.zeros((rows, SLOTS), jnp.float32)
    for k in range(top):
        same = ids[:, k : k + 1] == expert
        names = names + jnp.where(same, 1.0, 0.0)
        weight = weight + jnp.where(same, probs[:, k : k + 1], 0.0)
    before = lax.broadcasted_iota(jnp.int32, (rows, rows), 0) > lax.broadcasted_iota(
        jnp.int32, (rows, rows), 1
    )
    rank = dot(jnp.where(before, 1.0, 0.0).astype(jnp.bfloat16), names.astype(jnp.bfloat16), 1, 0)
    place = jnp.bitwise_and(lane, CAP - 1).astype(jnp.float32)
    hit = jnp.where(rank == place, names, 0.0)
    picked[...] = hit.astype(jnp.bfloat16)

    @pl.when(cut[0] == 0)
    def _():
        sent[...] = dot(hit.astype(jnp.bfloat16), tokens[...], 0, 0).astype(jnp.bfloat16)

    @pl.when(cut[0] != 0)
    def _():
        sent[...] = dot(
            hit * weight, grads[...].astype(jnp.float32), 0, 0, lax.Precision.HIGHEST
        ).astype(jnp.bfloat16)


def expert_kernel(
    cut, own, peer, gate_hbm, up_hbm, down_hbm, flat, backs, rows, grads, gate, up, down, sems
):
    def copies(rows_from, grads_from):
        pairs = ((rows_from, rows), (gate_hbm, gate), (up_hbm, up), (grads_from, grads), (down_hbm, down))
        return [pltpu.make_async_copy(a, b, sems.at[i]) for i, (a, b) in enumerate(pairs)]

    @pl.when(cut[0] == 0)
    def _():
        for copy in copies(own, peer):
            copy.start()

    @pl.when(cut[0] != 0)
    def _():
        for copy in copies(peer, own):
            copy.start()

    waits = copies(own, peer)
    for copy in waits[:2]:
        copy.wait()
    gate_val = dot(rows[...], gate[...], 1, 0)
    waits[2].wait()
    up_val = dot(rows[...], up[...], 1, 0)
    sigma = 1.0 / (1.0 + jnp.exp(-gate_val))
    activated = gate_val * sigma
    slope = sigma * (1.0 + gate_val * (1.0 - sigma))
    hidden = activated * up_val
    for copy in waits[3:]:
        copy.wait()
    back_hid = dot(grads[...], down[...], 1, 1)
    gate_back = back_hid * up_val * slope
    up_back = back_hid * activated
    width = rows.shape[1]
    units = hidden.shape[1]
    both = jnp.concatenate((gate_back, up_back), axis=1)
    backs[...] = both.astype(jnp.bfloat16)
    both_t = both.T.astype(jnp.bfloat16)
    hidden_t = hidden.T.astype(jnp.bfloat16)
    replicas = flat.shape[0]
    strip = units // replicas
    share = width // replicas
    for i in range(replicas):
        columns = slice(i * share, (i + 1) * share)
        two = dot(both_t, rows[:, columns], 1, 0).astype(jnp.bfloat16)
        three = dot(hidden_t, grads[:, columns], 1, 0).astype(jnp.bfloat16)
        per = share // 128
        for h in range(per):
            lanes = slice(h * 128, (h + 1) * 128)
            flat[i, h * 2 * units : (h + 1) * 2 * units, :] = two[:, lanes]
            start = 2 * per * units + (i * per + h) * strip
            for j in range(replicas):
                flat[j, start : start + strip, :] = three[j * strip : (j + 1) * strip, lanes]


def rows_kernel(cut, backs, gate, up, mine, other):
    half = mine.shape[1]
    units = gate.shape[1]

    def part(c):
        at = pl.ds(pl.multiple_of(c * half, half), half)
        return dot(backs[:, :units], gate[at, :], 1, 1) + dot(backs[:, units:], up[at, :], 1, 1)

    other[...] = part(1 - cut[0]).astype(jnp.bfloat16)
    mine[...] = part(cut[0])


def unpack_kernel(total, gate, up, down):
    units = gate.shape[1]
    per = gate.shape[0] // 128
    strip = down.shape[0]
    for h in range(per):
        at = h * 2 * units
        lanes = slice(h * 128, (h + 1) * 128)
        gate[lanes, :] = total[at : at + units, :].astype(jnp.float32).T.astype(jnp.bfloat16)
        up[lanes, :] = total[at + units : at + 2 * units, :].astype(jnp.float32).T.astype(jnp.bfloat16)
    base = per * 2 * units
    for j in range(down.shape[1] // 128):
        down[:, j * 128 : (j + 1) * 128] = total[base + j * strip : base + (j + 1) * strip, :]


def shards(tokens, out_grad, expert_ids, route_probs, gate_weight, up_weight, down_weight):
    rows, width = tokens.shape
    half = width // 2
    units = gate_weight.shape[2]
    replicas = lax.axis_size("dp")
    share = width // replicas
    strip = units // replicas
    cut = lax.axis_index("cuts").astype(jnp.int32).reshape(1)
    first = cut[0] == 0
    swap = [(0, 1), (1, 0)]
    w_gate, w_up, w_down = gate_weight[:, 0, :], up_weight[:, 0, :], down_weight[:, 0, :]
    bf16 = functools.partial(jax.ShapeDtypeStruct, dtype=jnp.bfloat16)

    sent, picked = pl.pallas_call(
        send_kernel,
        out_shape=(bf16((SLOTS, width)), bf16((rows, SLOTS))),
        in_specs=[SMEM] + [VMEM] * 4,
        out_specs=(VMEM, VMEM),
        compiler_params=PARAMS,
        name="send",
    )(cut, expert_ids, route_probs, tokens, out_grad)
    own = lax.all_to_all(
        sent.reshape(EXPERTS, CAP, width), "expert", split_axis=0, concat_axis=0, tiled=True
    ).reshape(SLOTS, width)
    peer = lax.ppermute(own, "cuts", swap)

    flat, backs = pl.pallas_call(
        expert_kernel,
        out_shape=(bf16((replicas, 3 * units * share // 128, 128)), bf16((SLOTS, 2 * units))),
        in_specs=[SMEM] + [ANY] * 5,
        out_specs=(VMEM, VMEM),
        scratch_shapes=[
            pltpu.VMEM((SLOTS, width), jnp.bfloat16),
            pltpu.VMEM((SLOTS, width), jnp.bfloat16),
            pltpu.VMEM((width, units), jnp.bfloat16),
            pltpu.VMEM((width, units), jnp.bfloat16),
            pltpu.VMEM((units, width), jnp.bfloat16),
            pltpu.SemaphoreType.DMA((5,)),
        ],
        compiler_params=PARAMS,
        name="expert",
    )(cut, own, peer, w_gate, w_up, w_down)
    total = lax.psum_scatter(flat, "dp", scatter_dimension=0, tiled=True)[0]

    mine, other = pl.pallas_call(
        rows_kernel,
        out_shape=(jax.ShapeDtypeStruct((SLOTS, half), jnp.float32), bf16((SLOTS, half))),
        in_specs=[SMEM] + [VMEM] * 3,
        out_specs=(VMEM, VMEM),
        compiler_params=PARAMS,
        name="rows",
    )(cut, backs, w_gate, w_up)
    mine = mine + lax.ppermute(other, "cuts", swap).astype(jnp.float32)
    returned = lax.all_to_all(
        mine.astype(jnp.bfloat16).reshape(EXPERTS, CAP, half),
        "expert", split_axis=0, concat_axis=0, tiled=True,
    ).reshape(SLOTS, half)
    result = dot(picked, returned, 1, 0).astype(jnp.bfloat16)

    gate_grad, up_grad, down_grad = pl.pallas_call(
        unpack_kernel,
        out_shape=(bf16((share, units)), bf16((share, units)), bf16((strip, width))),
        in_specs=[VMEM],
        out_specs=(VMEM,) * 3,
        compiler_params=PARAMS,
        name="unpack",
    )(total)
    return (result, gate_grad[:, None, :], up_grad[:, None, :], down_grad[:, None, :])


def solution(mesh):
    placed = (
        P(("expert", "dp"), None),
        P(("expert", "dp"), None),
        P(("expert", "dp"), None),
        P(("expert", "dp"), None),
        P(None, "expert", "cuts"),
        P(None, "expert", "cuts"),
        P("cuts", "expert", None),
    )
    return jax.shard_map(
        shards,
        mesh=mesh,
        in_specs=placed,
        out_specs=(
            P(("expert", "dp"), "cuts"),
            P("dp", "expert", "cuts"),
            P("dp", "expert", "cuts"),
            P(("cuts", "dp"), "expert", None),
        ),
        check_vma=False,
    )
```

```python
import functools

import jax
import jax.numpy as jnp
from jax import lax
from jax.experimental import pallas as pl
from jax.experimental.pallas import tpu as pltpu
from jax.sharding import PartitionSpec as P

EXPERTS = 64
CAP = 4
SLOTS = EXPERTS * CAP
VMEM = pl.BlockSpec(memory_space=pltpu.VMEM)
SMEM = pl.BlockSpec(memory_space=pltpu.SMEM)
ANY = pl.BlockSpec(memory_space=pl.ANY)
HBM = pl.BlockSpec(memory_space=pltpu.HBM)
PARAMS = pltpu.CompilerParams(vmem_limit_bytes=32 * 1024 * 1024)


def dot(a, b, da, db, precision=None):
    return lax.dot_general(
        a, b, (((da,), (db,)), ((), ())), precision=precision, preferred_element_type=jnp.float32
    )


def pack_kernel(cut, ids_hbm, probs_hbm, tokens, grads, packed, ids_t, probs_t, sems):
    top = ids_t.shape[0]
    width = tokens.shape[1]
    body = packed.at[:, pl.ds(0, width)]
    load_ids = pltpu.make_async_copy(ids_hbm, ids_t, sems.at[0])
    load_probs = pltpu.make_async_copy(probs_hbm, probs_t, sems.at[1])
    load_ids.start()
    load_probs.start()

    @pl.when(cut[0] == 0)
    def _():
        pltpu.make_async_copy(tokens, body, sems.at[2]).start()

    @pl.when(cut[0] != 0)
    def _():
        pltpu.make_async_copy(grads, body, sems.at[2]).start()

    load_ids.wait()
    load_probs.wait()
    probs = probs_t[...]
    high = probs.astype(jnp.bfloat16).astype(jnp.float32)
    middle = (probs - high).astype(jnp.bfloat16).astype(jnp.float32)
    low = probs - high - middle
    terms = jnp.concatenate((ids_t[...].astype(jnp.float32), high, middle, low), axis=0)
    row = lax.broadcasted_iota(jnp.int32, (4 * top, 128), 0)
    unit = jnp.where(row == lax.broadcasted_iota(jnp.int32, (4 * top, 128), 1), 1.0, 0.0)
    packed[:, width:] = dot(
        terms.astype(jnp.bfloat16), unit.astype(jnp.bfloat16), 0, 0
    ).astype(jnp.bfloat16)
    pltpu.make_async_copy(tokens, body, sems.at[2]).wait()


def ranks(names):
    rows = names.shape[0]
    before = lax.broadcasted_iota(jnp.int32, (rows, rows), 0) > lax.broadcasted_iota(
        jnp.int32, (rows, rows), 1
    )
    return dot(jnp.where(before, 1.0, 0.0).astype(jnp.bfloat16), names.astype(jnp.bfloat16), 1, 0)


def pick_kernel(place, own, behind, ahead, across, sent):
    rows, packed = own.shape
    width = sent.shape[1]
    f32 = jnp.float32
    blocks = (own, behind, ahead, across)
    source = jnp.concatenate([b[:, :width].astype(f32) for b in blocks], axis=0).astype(jnp.bfloat16)
    facts = jnp.concatenate([b[:, width:].astype(f32) for b in blocks], axis=0)
    total = 4 * rows
    group = place[1]
    token = lax.broadcasted_iota(jnp.int32, (total, SLOTS), 0)
    lane = lax.broadcasted_iota(jnp.int32, (total, SLOTS), 1)
    shift = jnp.where(
        token < rows, 0, jnp.where(token < 2 * rows, 3, jnp.where(token < 3 * rows, 1, 2))
    )
    block = jnp.bitwise_and(group + shift, 3)
    here = block == jnp.bitwise_and(lax.shift_right_logical(lane, 2), 3)
    expert = (group * 16 + lax.shift_right_logical(lane, 4)).astype(f32)
    names = jnp.zeros((total, SLOTS), f32)
    weight = jnp.zeros((total, SLOTS), f32)
    top = 8
    prob = facts[:, top : 2 * top] + facts[:, 2 * top : 3 * top] + facts[:, 3 * top : 4 * top]
    for k in range(top):
        same = jnp.logical_and(facts[:, k : k + 1] == expert, here)
        names = names + jnp.where(same, 1.0, 0.0)
        weight = weight + jnp.where(same, prob[:, k : k + 1], 0.0)
    slot = jnp.bitwise_and(lane, CAP - 1).astype(f32)
    hit = jnp.where(ranks(names) == slot, names, 0.0)

    @pl.when(place[0] == 0)
    def _():
        sent[...] = dot(hit.astype(jnp.bfloat16), source, 0, 0).astype(jnp.bfloat16)

    @pl.when(place[0] != 0)
    def _():
        factor = hit * weight
        high = factor.astype(jnp.bfloat16)
        middle = (factor - high.astype(f32)).astype(jnp.bfloat16)
        low = (factor - high.astype(f32) - middle.astype(f32)).astype(jnp.bfloat16)
        sent[...] = (
            dot(high, source, 0, 0) + (dot(middle, source, 0, 0) + dot(low, source, 0, 0))
        ).astype(jnp.bfloat16)


def combine_kernel(ids_t, returned, out):
    top, rows = ids_t.shape
    unit = jnp.where(
        lax.broadcasted_iota(jnp.int32, (top, top), 0) == lax.broadcasted_iota(jnp.int32, (top, top), 1),
        1.0, 0.0,
    )
    ids = dot(ids_t[...].astype(jnp.bfloat16), unit.astype(jnp.bfloat16), 0, 0)
    lane = lax.broadcasted_iota(jnp.int32, (rows, SLOTS), 1)
    expert = lax.shift_right_logical(lane, 2).astype(jnp.float32)
    names = jnp.zeros((rows, SLOTS), jnp.float32)
    for k in range(top):
        names = names + jnp.where(ids[:, k : k + 1] == expert, 1.0, 0.0)
    slot = jnp.bitwise_and(lane, CAP - 1).astype(jnp.float32)
    hit = jnp.where(ranks(names) == slot, names, 0.0)
    out[...] = dot(hit.astype(jnp.bfloat16), returned[...], 1, 0).astype(jnp.bfloat16)


def expert_kernel(
    place, own, peer, gate_hbm, up_hbm, down_hbm, flat_hbm, backs,
    rows, grads, gate, up, down, flat, sems, out_sems,
):
    def copies(rows_from, grads_from):
        pairs = ((rows_from, rows), (gate_hbm, gate), (up_hbm, up), (grads_from, grads), (down_hbm, down))
        return [pltpu.make_async_copy(a, b, sems.at[i]) for i, (a, b) in enumerate(pairs)]

    @pl.when(place[0] == 0)
    def _():
        for copy in copies(own, peer):
            copy.start()

    @pl.when(place[0] != 0)
    def _():
        for copy in copies(peer, own):
            copy.start()

    waits = copies(own, peer)
    for copy in waits[:2]:
        copy.wait()
    gate_val = dot(rows[...], gate[...], 1, 0)
    waits[2].wait()
    up_val = dot(rows[...], up[...], 1, 0)
    sigma = 1.0 / (1.0 + jnp.exp(-gate_val))
    activated = gate_val * sigma
    slope = sigma * (1.0 + gate_val * (1.0 - sigma))
    hidden_t = (activated * up_val).T.astype(jnp.bfloat16)
    width = rows.shape[1]
    units = gate.shape[1]
    replicas = flat.shape[0]
    strip = units // replicas
    share = width // replicas
    per = share // 128
    for copy in waits[3:]:
        copy.wait()
    back_hid = dot(grads[...], down[...], 1, 1)
    for i in range(replicas):
        columns = slice(i * share, (i + 1) * share)
        part = dot(hidden_t, grads[:, columns], 1, 0).astype(jnp.bfloat16)
        for h in range(per):
            lanes = slice(h * 128, (h + 1) * 128)
            start = 2 * per * units + (i * per + h) * strip
            for j in range(replicas):
                flat[j, start : start + strip, :] = part[j * strip : (j + 1) * strip, lanes]
    both = jnp.concatenate((back_hid * up_val * slope, back_hid * activated), axis=1)
    backs[...] = both.astype(jnp.bfloat16)
    both_t = both.T.astype(jnp.bfloat16)
    outs = [
        pltpu.make_async_copy(flat.at[i], flat_hbm.at[i], out_sems.at[i]) for i in range(replicas)
    ]
    for i in range(replicas):
        columns = slice(i * share, (i + 1) * share)
        part = dot(both_t, rows[:, columns], 1, 0).astype(jnp.bfloat16)
        for h in range(per):
            flat[i, h * 2 * units : (h + 1) * 2 * units, :] = part[:, h * 128 : (h + 1) * 128]
        outs[i].start()
    for copy in outs:
        copy.wait()


def rows_kernel(cut, backs, gate, up, mine, other):
    half = mine.shape[1]
    units = gate.shape[1]

    def part(c):
        at = pl.ds(pl.multiple_of(c * half, half), half)
        return dot(backs[:, :units], gate[at, :], 1, 1) + dot(backs[:, units:], up[at, :], 1, 1)

    other[...] = part(1 - cut[0]).astype(jnp.bfloat16)
    mine[...] = part(cut[0])


def unpack_kernel(total, gate, up, down):
    units = gate.shape[1]
    per = gate.shape[0] // 128
    strip = down.shape[0]
    for h in range(per):
        at = h * 2 * units
        lanes = slice(h * 128, (h + 1) * 128)
        gate[lanes, :] = total[at : at + units, :].astype(jnp.float32).T.astype(jnp.bfloat16)
        up[lanes, :] = total[at + units : at + 2 * units, :].astype(jnp.float32).T.astype(jnp.bfloat16)
    base = per * 2 * units
    for j in range(down.shape[1] // 128):
        down[:, j * 128 : (j + 1) * 128] = total[base + j * strip : base + (j + 1) * strip, :]


def shards(tokens, out_grad, expert_ids, route_probs, gate_weight, up_weight, down_weight):
    rows, width = tokens.shape
    half = width // 2
    units = gate_weight.shape[2]
    replicas = lax.axis_size("dp")
    share = width // replicas
    strip = units // replicas
    cut = lax.axis_index("cuts").astype(jnp.int32).reshape(1)
    place = jnp.stack((lax.axis_index("cuts"), lax.axis_index("expert") // 16)).astype(jnp.int32)
    swap = [(0, 1), (1, 0)]
    w_gate, w_up, w_down = gate_weight[:, 0, :], up_weight[:, 0, :], down_weight[:, 0, :]
    bf16 = functools.partial(jax.ShapeDtypeStruct, dtype=jnp.bfloat16)
    ids_t, probs_t = expert_ids.T, route_probs.T

    packed = pl.pallas_call(
        pack_kernel,
        out_shape=bf16((rows, width + 128)),
        in_specs=[SMEM] + [ANY] * 4,
        out_specs=VMEM,
        scratch_shapes=[
            pltpu.VMEM(ids_t.shape, jnp.int32),
            pltpu.VMEM(probs_t.shape, jnp.float32),
            pltpu.SemaphoreType.DMA((3,)),
        ],
        compiler_params=pltpu.CompilerParams(vmem_limit_bytes=60 * 1024 * 1024),
        name="pack",
    )(cut, ids_t, probs_t, tokens, out_grad)
    up_by = [(i, (i + 16) % EXPERTS) for i in range(EXPERTS)]
    down_by = [(j, i) for i, j in up_by]
    behind = lax.ppermute(packed, "expert", up_by)
    ahead = lax.ppermute(packed, "expert", down_by)
    across = lax.ppermute(packed, "expert", [(i, (i + 32) % EXPERTS) for i in range(EXPERTS)])
    sent = pl.pallas_call(
        pick_kernel,
        out_shape=bf16((SLOTS, width)),
        in_specs=[SMEM] + [VMEM] * 4,
        out_specs=VMEM,
        compiler_params=PARAMS,
        name="pick",
    )(place, packed, behind, ahead, across)
    quarters = [[q * 16 + i for i in range(16)] for q in range(4)]
    own = lax.all_to_all(
        sent.reshape(16, 4 * CAP, width), "expert", split_axis=0, concat_axis=0, tiled=True,
        axis_index_groups=quarters,
    ).reshape(SLOTS, width)
    peer = lax.ppermute(own, "cuts", swap)

    flat, backs = pl.pallas_call(
        expert_kernel,
        out_shape=(bf16((replicas, 3 * units * share // 128, 128)), bf16((SLOTS, 2 * units))),
        in_specs=[SMEM, HBM] + [ANY] * 4,
        out_specs=(HBM, VMEM),
        scratch_shapes=[
            pltpu.VMEM((SLOTS, width), jnp.bfloat16),
            pltpu.VMEM((SLOTS, width), jnp.bfloat16),
            pltpu.VMEM((width, units), jnp.bfloat16),
            pltpu.VMEM((width, units), jnp.bfloat16),
            pltpu.VMEM((units, width), jnp.bfloat16),
            pltpu.VMEM((replicas, 3 * units * share // 128, 128), jnp.bfloat16),
            pltpu.SemaphoreType.DMA((5,)),
            pltpu.SemaphoreType.DMA((replicas,)),
        ],
        compiler_params=pltpu.CompilerParams(vmem_limit_bytes=48 * 1024 * 1024),
        name="expert",
    )(cut, own, peer, w_gate, w_up, w_down)
    total = lax.psum_scatter(flat, "dp", scatter_dimension=0, tiled=True)[0]

    mine, other = pl.pallas_call(
        rows_kernel,
        out_shape=(jax.ShapeDtypeStruct((SLOTS, half), jnp.float32), bf16((SLOTS, half))),
        in_specs=[SMEM] + [VMEM] * 3,
        out_specs=(VMEM, VMEM),
        compiler_params=PARAMS,
        name="rows",
    )(cut, backs, w_gate, w_up)
    mine = mine + lax.ppermute(other, "cuts", swap).astype(jnp.float32)
    returned = lax.all_to_all(
        mine.astype(jnp.bfloat16).reshape(16, 4, CAP, half).transpose(1, 0, 2, 3)
        .reshape(EXPERTS, CAP, half),
        "expert", split_axis=0, concat_axis=0, tiled=True,
    ).reshape(SLOTS, half)
    result = pl.pallas_call(
        combine_kernel,
        out_shape=bf16((rows, half)),
        in_specs=[VMEM] * 2,
        out_specs=VMEM,
        compiler_params=PARAMS,
        name="combine",
    )(ids_t, returned)

    gate_grad, up_grad, down_grad = pl.pallas_call(
        unpack_kernel,
        out_shape=(bf16((share, units)), bf16((share, units)), bf16((strip, width))),
        in_specs=[VMEM],
        out_specs=(VMEM,) * 3,
        compiler_params=PARAMS,
        name="unpack",
    )(total)
    return (result, gate_grad[:, None, :], up_grad[:, None, :], down_grad[:, None, :])


def solution(mesh):
    placed = (
        P(("expert", "dp"), None),
        P(("expert", "dp"), None),
        P(("expert", "dp"), None),
        P(("expert", "dp"), None),
        P(None, "expert", "cuts"),
        P(None, "expert", "cuts"),
        P("cuts", "expert", None),
    )
    return jax.shard_map(
        shards,
        mesh=mesh,
        in_specs=placed,
        out_specs=(
            P(("expert", "dp"), "cuts"),
            P("dp", "expert", "cuts"),
            P("dp", "expert", "cuts"),
            P(("cuts", "dp"), "expert", None),
        ),
        check_vma=False,
    )
```

```python
import functools

import jax
import jax.numpy as jnp
from jax import lax
from jax.experimental import pallas as pl
from jax.experimental.pallas import tpu as pltpu
from jax.sharding import PartitionSpec as P

EXPERTS = 64
CAP = 4
SLOTS = EXPERTS * CAP
VMEM = pl.BlockSpec(memory_space=pltpu.VMEM)
SMEM = pl.BlockSpec(memory_space=pltpu.SMEM)
ANY = pl.BlockSpec(memory_space=pl.ANY)
HBM = pl.BlockSpec(memory_space=pltpu.HBM)
PARAMS = pltpu.CompilerParams(vmem_limit_bytes=32 * 1024 * 1024)


def dot(a, b, da, db, precision=None):
    return lax.dot_general(
        a, b, (((da,), (db,)), ((), ())), precision=precision, preferred_element_type=jnp.float32
    )


def pack_kernel(cut, ids_hbm, probs_hbm, tokens, grads, packed, ids_t, probs_t, sems):
    top = ids_t.shape[0]
    width = tokens.shape[1]
    body = packed.at[:, pl.ds(0, width)]
    load_ids = pltpu.make_async_copy(ids_hbm, ids_t, sems.at[0])
    load_probs = pltpu.make_async_copy(probs_hbm, probs_t, sems.at[1])
    load_ids.start()
    load_probs.start()

    @pl.when(cut[0] == 0)
    def _():
        pltpu.make_async_copy(tokens, body, sems.at[2]).start()

    @pl.when(cut[0] != 0)
    def _():
        pltpu.make_async_copy(grads, body, sems.at[2]).start()

    load_ids.wait()
    load_probs.wait()
    probs = probs_t[...]
    high = probs.astype(jnp.bfloat16).astype(jnp.float32)
    middle = (probs - high).astype(jnp.bfloat16).astype(jnp.float32)
    low = probs - high - middle
    terms = jnp.concatenate((ids_t[...].astype(jnp.float32), high, middle, low), axis=0)
    row = lax.broadcasted_iota(jnp.int32, (4 * top, 128), 0)
    unit = jnp.where(row == lax.broadcasted_iota(jnp.int32, (4 * top, 128), 1), 1.0, 0.0)
    packed[:, width:] = dot(
        terms.astype(jnp.bfloat16), unit.astype(jnp.bfloat16), 0, 0
    ).astype(jnp.bfloat16)
    pltpu.make_async_copy(tokens, body, sems.at[2]).wait()


def ranks(names):
    rows = names.shape[0]
    before = lax.broadcasted_iota(jnp.int32, (rows, rows), 0) > lax.broadcasted_iota(
        jnp.int32, (rows, rows), 1
    )
    return dot(jnp.where(before, 1.0, 0.0).astype(jnp.bfloat16), names.astype(jnp.bfloat16), 1, 0)


def pick_kernel(place, own, behind, ahead, across, sent):
    rows, packed = own.shape
    width = sent.shape[1]
    f32 = jnp.float32
    blocks = (own, behind, ahead, across)
    source = jnp.concatenate([b[:, :width].astype(f32) for b in blocks], axis=0).astype(jnp.bfloat16)
    facts = jnp.concatenate([b[:, width:].astype(f32) for b in blocks], axis=0)
    total = 4 * rows
    group = place[1]
    token = lax.broadcasted_iota(jnp.int32, (total, SLOTS), 0)
    lane = lax.broadcasted_iota(jnp.int32, (total, SLOTS), 1)
    shift = jnp.where(
        token < rows, 0, jnp.where(token < 2 * rows, 3, jnp.where(token < 3 * rows, 1, 2))
    )
    block = jnp.bitwise_and(group + shift, 3)
    here = block == jnp.bitwise_and(lax.shift_right_logical(lane, 2), 3)
    expert = (group * 16 + lax.shift_right_logical(lane, 4)).astype(f32)
    names = jnp.zeros((total, SLOTS), f32)
    weight = jnp.zeros((total, SLOTS), f32)
    top = 8
    prob = facts[:, top : 2 * top] + facts[:, 2 * top : 3 * top] + facts[:, 3 * top : 4 * top]
    for k in range(top):
        same = jnp.logical_and(facts[:, k : k + 1] == expert, here)
        names = names + jnp.where(same, 1.0, 0.0)
        weight = weight + jnp.where(same, prob[:, k : k + 1], 0.0)
    slot = jnp.bitwise_and(lane, CAP - 1).astype(f32)
    hit = jnp.where(ranks(names) == slot, names, 0.0)

    @pl.when(place[0] == 0)
    def _():
        sent[...] = dot(hit.astype(jnp.bfloat16), source, 0, 0).astype(jnp.bfloat16)

    @pl.when(place[0] != 0)
    def _():
        factor = hit * weight
        high = factor.astype(jnp.bfloat16)
        middle = (factor - high.astype(f32)).astype(jnp.bfloat16)
        low = (factor - high.astype(f32) - middle.astype(f32)).astype(jnp.bfloat16)
        sent[...] = (
            dot(high, source, 0, 0) + (dot(middle, source, 0, 0) + dot(low, source, 0, 0))
        ).astype(jnp.bfloat16)


def combine_kernel(ids_t, returned, out):
    top, rows = ids_t.shape
    unit = jnp.where(
        lax.broadcasted_iota(jnp.int32, (top, top), 0) == lax.broadcasted_iota(jnp.int32, (top, top), 1),
        1.0, 0.0,
    )
    ids = dot(ids_t[...].astype(jnp.bfloat16), unit.astype(jnp.bfloat16), 0, 0)
    lane = lax.broadcasted_iota(jnp.int32, (rows, SLOTS), 1)
    expert = lax.shift_right_logical(lane, 2).astype(jnp.float32)
    names = jnp.zeros((rows, SLOTS), jnp.float32)
    for k in range(top):
        names = names + jnp.where(ids[:, k : k + 1] == expert, 1.0, 0.0)
    slot = jnp.bitwise_and(lane, CAP - 1).astype(jnp.float32)
    hit = jnp.where(ranks(names) == slot, names, 0.0)
    out[...] = dot(hit.astype(jnp.bfloat16), returned[...], 1, 0).astype(jnp.bfloat16)


def expert_kernel(
    place, own, peer, gate_hbm, up_hbm, down_hbm, flat_hbm, turned, backs,
    rows, grads, gate, up, down, flat, sems, out_sems,
):
    me = place[1]

    def copies(rows_from, grads_from):
        pairs = ((rows_from, rows), (gate_hbm, gate), (up_hbm, up), (grads_from, grads), (down_hbm, down))
        return [pltpu.make_async_copy(a, b, sems.at[i]) for i, (a, b) in enumerate(pairs)]

    @pl.when(place[0] == 0)
    def _():
        for copy in copies(own, peer):
            copy.start()

    @pl.when(place[0] != 0)
    def _():
        for copy in copies(peer, own):
            copy.start()

    waits = copies(own, peer)
    for copy in waits[:2]:
        copy.wait()
    gate_val = dot(rows[...], gate[...], 1, 0)
    waits[2].wait()
    up_val = dot(rows[...], up[...], 1, 0)
    sigma = 1.0 / (1.0 + jnp.exp(-gate_val))
    activated = gate_val * sigma
    slope = sigma * (1.0 + gate_val * (1.0 - sigma))
    hidden_t = (activated * up_val).T.astype(jnp.bfloat16)
    width = rows.shape[1]
    units = gate.shape[1]
    replicas = flat.shape[0]
    strip = units // replicas
    share = width // replicas
    per = share // 128
    for copy in waits[3:]:
        copy.wait()
    back_hid = dot(grads[...], down[...], 1, 1)
    for i in range(replicas):
        columns = slice(i * share, (i + 1) * share)
        part = dot(hidden_t, grads[:, columns], 1, 0).astype(jnp.bfloat16)
        for h in range(per):
            lanes = slice(h * 128, (h + 1) * 128)
            start = (i * per + h) * strip
            for j in range(replicas):
                ahead = jnp.bitwise_and(j - me + replicas, replicas - 1)
                turned[ahead, start : start + strip, :] = part[j * strip : (j + 1) * strip, lanes]
    both = jnp.concatenate((back_hid * up_val * slope, back_hid * activated), axis=1)
    backs[...] = both.astype(jnp.bfloat16)
    both_t = both.T.astype(jnp.bfloat16)
    outs = [
        pltpu.make_async_copy(flat.at[i], flat_hbm.at[i], out_sems.at[i]) for i in range(replicas)
    ]
    for i in range(replicas):
        columns = slice(i * share, (i + 1) * share)
        part = dot(both_t, rows[:, columns], 1, 0).astype(jnp.bfloat16)
        for h in range(per):
            flat[i, h * 2 * units : (h + 1) * 2 * units, :] = part[:, h * 128 : (h + 1) * 128]
        outs[i].start()
    for copy in outs:
        copy.wait()


def rows_kernel(cut, backs, gate, up, mine, other):
    half = mine.shape[1]
    units = gate.shape[1]

    def part(c):
        at = pl.ds(pl.multiple_of(c * half, half), half)
        return dot(backs[:, :units], gate[at, :], 1, 1) + dot(backs[:, units:], up[at, :], 1, 1)

    other[...] = part(1 - cut[0]).astype(jnp.bfloat16)
    mine[...] = part(cut[0])


def unpack_kernel(total, down_total, gate, up, down):
    units = gate.shape[1]
    per = gate.shape[0] // 128
    strip = down.shape[0]
    for h in range(per):
        at = h * 2 * units
        lanes = slice(h * 128, (h + 1) * 128)
        gate[lanes, :] = total[at : at + units, :].astype(jnp.float32).T.astype(jnp.bfloat16)
        up[lanes, :] = total[at + units : at + 2 * units, :].astype(jnp.float32).T.astype(jnp.bfloat16)
    for j in range(down.shape[1] // 128):
        down[:, j * 128 : (j + 1) * 128] = down_total[j * strip : (j + 1) * strip, :]


def ring_sum(turned):
    size = turned.shape[0]
    half = turned.shape[1] // 2
    onward = [(i, (i + 1) % size) for i in range(size)]
    back = [(j, i) for i, j in onward]

    def add(a, b):
        return (a.astype(jnp.float32) + b.astype(jnp.float32)).astype(jnp.bfloat16)

    far = turned[size // 2]
    right = lax.ppermute(far[:half], "dp", onward)
    left = lax.ppermute(far[half:], "dp", back)
    for step in range(size // 2 - 1, 0, -1):
        r, l = turned[step], turned[size - step]
        if step == size // 2 - 1:
            right = jnp.concatenate((add(right, r[:half]), r[half:]), axis=0)
            left = jnp.concatenate((l[:half], add(left, l[half:])), axis=0)
        else:
            right, left = add(right, r), add(left, l)
        right = lax.ppermute(right, "dp", onward)
        left = lax.ppermute(left, "dp", back)
    return (
        turned[0].astype(jnp.float32) + right.astype(jnp.float32) + left.astype(jnp.float32)
    ).astype(jnp.bfloat16)


def shards(tokens, out_grad, expert_ids, route_probs, gate_weight, up_weight, down_weight):
    rows, width = tokens.shape
    half = width // 2
    units = gate_weight.shape[2]
    replicas = lax.axis_size("dp")
    share = width // replicas
    strip = units // replicas
    cut = lax.axis_index("cuts").astype(jnp.int32).reshape(1)
    place = jnp.stack((lax.axis_index("cuts"), lax.axis_index("expert") // 16)).astype(jnp.int32)
    swap = [(0, 1), (1, 0)]
    w_gate, w_up, w_down = gate_weight[:, 0, :], up_weight[:, 0, :], down_weight[:, 0, :]
    bf16 = functools.partial(jax.ShapeDtypeStruct, dtype=jnp.bfloat16)
    ids_t, probs_t = expert_ids.T, route_probs.T

    packed = pl.pallas_call(
        pack_kernel,
        out_shape=bf16((rows, width + 128)),
        in_specs=[SMEM] + [ANY] * 4,
        out_specs=VMEM,
        scratch_shapes=[
            pltpu.VMEM(ids_t.shape, jnp.int32),
            pltpu.VMEM(probs_t.shape, jnp.float32),
            pltpu.SemaphoreType.DMA((3,)),
        ],
        compiler_params=pltpu.CompilerParams(vmem_limit_bytes=60 * 1024 * 1024),
        name="pack",
    )(cut, ids_t, probs_t, tokens, out_grad)
    up_by = [(i, (i + 16) % EXPERTS) for i in range(EXPERTS)]
    down_by = [(j, i) for i, j in up_by]
    behind = lax.ppermute(packed, "expert", up_by)
    ahead = lax.ppermute(packed, "expert", down_by)
    across = lax.ppermute(packed, "expert", [(i, (i + 32) % EXPERTS) for i in range(EXPERTS)])
    sent = pl.pallas_call(
        pick_kernel,
        out_shape=bf16((SLOTS, width)),
        in_specs=[SMEM] + [VMEM] * 4,
        out_specs=VMEM,
        compiler_params=PARAMS,
        name="pick",
    )(place, packed, behind, ahead, across)
    quarters = [[q * 16 + i for i in range(16)] for q in range(4)]
    own = lax.all_to_all(
        sent.reshape(16, 4 * CAP, width), "expert", split_axis=0, concat_axis=0, tiled=True,
        axis_index_groups=quarters,
    ).reshape(SLOTS, width)
    peer = lax.ppermute(own, "cuts", swap)

    flat, turned, backs = pl.pallas_call(
        expert_kernel,
        out_shape=(
            bf16((replicas, 2 * units * share // 128, 128)),
            bf16((replicas, strip * width // 128, 128)),
            bf16((SLOTS, 2 * units)),
        ),
        in_specs=[SMEM, HBM] + [ANY] * 4,
        out_specs=(HBM, VMEM, VMEM),
        scratch_shapes=[
            pltpu.VMEM((SLOTS, width), jnp.bfloat16),
            pltpu.VMEM((SLOTS, width), jnp.bfloat16),
            pltpu.VMEM((width, units), jnp.bfloat16),
            pltpu.VMEM((width, units), jnp.bfloat16),
            pltpu.VMEM((units, width), jnp.bfloat16),
            pltpu.VMEM((replicas, 2 * units * share // 128, 128), jnp.bfloat16),
            pltpu.SemaphoreType.DMA((5,)),
            pltpu.SemaphoreType.DMA((replicas,)),
        ],
        compiler_params=pltpu.CompilerParams(vmem_limit_bytes=46 * 1024 * 1024),
        name="expert",
    )(
        jnp.stack((lax.axis_index("cuts"), lax.axis_index("dp"))).astype(jnp.int32),
        own, peer, w_gate, w_up, w_down,
    )
    down_total = ring_sum(turned)
    total = lax.psum_scatter(flat, "dp", scatter_dimension=0, tiled=True)[0]

    mine, other = pl.pallas_call(
        rows_kernel,
        out_shape=(jax.ShapeDtypeStruct((SLOTS, half), jnp.float32), bf16((SLOTS, half))),
        in_specs=[SMEM] + [VMEM] * 3,
        out_specs=(VMEM, VMEM),
        compiler_params=PARAMS,
        name="rows",
    )(cut, backs, w_gate, w_up)
    mine = mine + lax.ppermute(other, "cuts", swap).astype(jnp.float32)
    returned = lax.all_to_all(
        mine.astype(jnp.bfloat16).reshape(16, 4, CAP, half).transpose(1, 0, 2, 3)
        .reshape(EXPERTS, CAP, half),
        "expert", split_axis=0, concat_axis=0, tiled=True,
    ).reshape(SLOTS, half)
    result = pl.pallas_call(
        combine_kernel,
        out_shape=bf16((rows, half)),
        in_specs=[VMEM] * 2,
        out_specs=VMEM,
        compiler_params=PARAMS,
        name="combine",
    )(ids_t, returned)

    gate_grad, up_grad, down_grad = pl.pallas_call(
        unpack_kernel,
        out_shape=(bf16((share, units)), bf16((share, units)), bf16((strip, width))),
        in_specs=[VMEM] * 2,
        out_specs=(VMEM,) * 3,
        compiler_params=PARAMS,
        name="unpack",
    )(total, down_total)
    return (result, gate_grad[:, None, :], up_grad[:, None, :], down_grad[:, None, :])


def solution(mesh):
    placed = (
        P(("expert", "dp"), None),
        P(("expert", "dp"), None),
        P(("expert", "dp"), None),
        P(("expert", "dp"), None),
        P(None, "expert", "cuts"),
        P(None, "expert", "cuts"),
        P("cuts", "expert", None),
    )
    return jax.shard_map(
        shards,
        mesh=mesh,
        in_specs=placed,
        out_specs=(
            P(("expert", "dp"), "cuts"),
            P("dp", "expert", "cuts"),
            P("dp", "expert", "cuts"),
            P(("cuts", "dp"), "expert", None),
        ),
        check_vma=False,
    )
```

```python
import functools

import jax
import jax.numpy as jnp
from jax import lax
from jax.experimental import pallas as pl
from jax.experimental.pallas import tpu as pltpu
from jax.sharding import PartitionSpec as P

EXPERTS = 64
CAP = 4
SLOTS = EXPERTS * CAP
VMEM = pl.BlockSpec(memory_space=pltpu.VMEM)
SMEM = pl.BlockSpec(memory_space=pltpu.SMEM)
ANY = pl.BlockSpec(memory_space=pl.ANY)
HBM = pl.BlockSpec(memory_space=pltpu.HBM)
PARAMS = pltpu.CompilerParams(vmem_limit_bytes=32 * 1024 * 1024)


def dot(a, b, da, db, precision=None):
    return lax.dot_general(
        a, b, (((da,), (db,)), ((), ())), precision=precision, preferred_element_type=jnp.float32
    )


def pack_kernel(cut, ids_hbm, probs_hbm, tokens, grads, packed, ids_t, probs_t, sems):
    top = ids_t.shape[0]
    width = tokens.shape[1]
    body = packed.at[:, pl.ds(0, width)]
    load_ids = pltpu.make_async_copy(ids_hbm, ids_t, sems.at[0])
    load_probs = pltpu.make_async_copy(probs_hbm, probs_t, sems.at[1])
    load_ids.start()
    load_probs.start()

    @pl.when(cut[0] == 0)
    def _():
        pltpu.make_async_copy(tokens, body, sems.at[2]).start()

    @pl.when(cut[0] != 0)
    def _():
        pltpu.make_async_copy(grads, body, sems.at[2]).start()

    load_ids.wait()
    load_probs.wait()
    probs = probs_t[...]
    high = probs.astype(jnp.bfloat16).astype(jnp.float32)
    middle = (probs - high).astype(jnp.bfloat16).astype(jnp.float32)
    low = probs - high - middle
    terms = jnp.concatenate((ids_t[...].astype(jnp.float32), high, middle, low), axis=0)
    row = lax.broadcasted_iota(jnp.int32, (4 * top, 128), 0)
    unit = jnp.where(row == lax.broadcasted_iota(jnp.int32, (4 * top, 128), 1), 1.0, 0.0)
    packed[:, width:] = dot(
        terms.astype(jnp.bfloat16), unit.astype(jnp.bfloat16), 0, 0
    ).astype(jnp.bfloat16)
    pltpu.make_async_copy(tokens, body, sems.at[2]).wait()


def ranks(names):
    rows = names.shape[0]
    before = lax.broadcasted_iota(jnp.int32, (rows, rows), 0) > lax.broadcasted_iota(
        jnp.int32, (rows, rows), 1
    )
    return dot(jnp.where(before, 1.0, 0.0).astype(jnp.bfloat16), names.astype(jnp.bfloat16), 1, 0)


def pick_kernel(place, own, behind, ahead, across, sent):
    rows, packed = own.shape
    width = sent.shape[1]
    f32 = jnp.float32
    blocks = (own, behind, ahead, across)
    source = jnp.concatenate([b[:, :width].astype(f32) for b in blocks], axis=0).astype(jnp.bfloat16)
    facts = jnp.concatenate([b[:, width:].astype(f32) for b in blocks], axis=0)
    total = 4 * rows
    group = place[1]
    token = lax.broadcasted_iota(jnp.int32, (total, SLOTS), 0)
    lane = lax.broadcasted_iota(jnp.int32, (total, SLOTS), 1)
    shift = jnp.where(
        token < rows, 0, jnp.where(token < 2 * rows, 3, jnp.where(token < 3 * rows, 1, 2))
    )
    block = jnp.bitwise_and(group + shift, 3)
    here = block == jnp.bitwise_and(lax.shift_right_logical(lane, 2), 3)
    expert = (group * 16 + lax.shift_right_logical(lane, 4)).astype(f32)
    names = jnp.zeros((total, SLOTS), f32)
    weight = jnp.zeros((total, SLOTS), f32)
    top = 8
    prob = facts[:, top : 2 * top] + facts[:, 2 * top : 3 * top] + facts[:, 3 * top : 4 * top]
    for k in range(top):
        same = jnp.logical_and(facts[:, k : k + 1] == expert, here)
        names = names + jnp.where(same, 1.0, 0.0)
        weight = weight + jnp.where(same, prob[:, k : k + 1], 0.0)
    slot = jnp.bitwise_and(lane, CAP - 1).astype(f32)
    hit = jnp.where(ranks(names) == slot, names, 0.0)

    @pl.when(place[0] == 0)
    def _():
        sent[...] = dot(hit.astype(jnp.bfloat16), source, 0, 0).astype(jnp.bfloat16)

    @pl.when(place[0] != 0)
    def _():
        factor = hit * weight
        high = factor.astype(jnp.bfloat16)
        middle = (factor - high.astype(f32)).astype(jnp.bfloat16)
        low = (factor - high.astype(f32) - middle.astype(f32)).astype(jnp.bfloat16)
        sent[...] = (
            dot(high, source, 0, 0) + (dot(middle, source, 0, 0) + dot(low, source, 0, 0))
        ).astype(jnp.bfloat16)


def combine_kernel(ids_t, returned, out):
    top, rows = ids_t.shape
    unit = jnp.where(
        lax.broadcasted_iota(jnp.int32, (top, top), 0) == lax.broadcasted_iota(jnp.int32, (top, top), 1),
        1.0, 0.0,
    )
    ids = dot(ids_t[...].astype(jnp.bfloat16), unit.astype(jnp.bfloat16), 0, 0)
    lane = lax.broadcasted_iota(jnp.int32, (rows, SLOTS), 1)
    expert = lax.shift_right_logical(lane, 2).astype(jnp.float32)
    names = jnp.zeros((rows, SLOTS), jnp.float32)
    for k in range(top):
        names = names + jnp.where(ids[:, k : k + 1] == expert, 1.0, 0.0)
    slot = jnp.bitwise_and(lane, CAP - 1).astype(jnp.float32)
    hit = jnp.where(ranks(names) == slot, names, 0.0)
    out[...] = dot(hit.astype(jnp.bfloat16), returned[...], 1, 0).astype(jnp.bfloat16)


def expert_kernel(place, own, peer, gate, up, down, flat_hbm, backs, rows, grads, flat, out_sems):
    @pl.when(place[0] == 0)
    def _():
        rows[...] = own[...]
        grads[...] = peer[...]

    @pl.when(place[0] != 0)
    def _():
        rows[...] = peer[...]
        grads[...] = own[...]

    gate_val = dot(rows[...], gate[...], 1, 0)
    up_val = dot(rows[...], up[...], 1, 0)
    sigma = 1.0 / (1.0 + jnp.exp(-gate_val))
    activated = gate_val * sigma
    slope = sigma * (1.0 + gate_val * (1.0 - sigma))
    hidden_t = (activated * up_val).T.astype(jnp.bfloat16)
    width = rows.shape[1]
    units = gate.shape[1]
    replicas = flat.shape[0]
    strip = units // replicas
    share = width // replicas
    per = share // 128
    back_hid = dot(grads[...], down[...], 1, 1)
    for i in range(replicas):
        columns = slice(i * share, (i + 1) * share)
        part = dot(hidden_t, grads[:, columns], 1, 0).astype(jnp.bfloat16)
        for h in range(per):
            lanes = slice(h * 128, (h + 1) * 128)
            start = 2 * per * units + (i * per + h) * strip
            for j in range(replicas):
                flat[j, start : start + strip, :] = part[j * strip : (j + 1) * strip, lanes]
    both = jnp.concatenate((back_hid * up_val * slope, back_hid * activated), axis=1)
    backs[...] = both.astype(jnp.bfloat16)
    both_t = both.T.astype(jnp.bfloat16)
    outs = [
        pltpu.make_async_copy(flat.at[i], flat_hbm.at[i], out_sems.at[i]) for i in range(replicas)
    ]
    for i in range(replicas):
        columns = slice(i * share, (i + 1) * share)
        part = dot(both_t, rows[:, columns], 1, 0).astype(jnp.bfloat16)
        for h in range(per):
            flat[i, h * 2 * units : (h + 1) * 2 * units, :] = part[:, h * 128 : (h + 1) * 128]
        outs[i].start()
    for copy in outs:
        copy.wait()


def rows_kernel(cut, backs, gate, up, mine, other):
    half = mine.shape[1]
    units = gate.shape[1]

    def part(c):
        at = pl.ds(pl.multiple_of(c * half, half), half)
        return dot(backs[:, :units], gate[at, :], 1, 1) + dot(backs[:, units:], up[at, :], 1, 1)

    other[...] = part(1 - cut[0]).astype(jnp.bfloat16)
    mine[...] = part(cut[0])


def unpack_kernel(total, gate, up, down):
    units = gate.shape[1]
    per = gate.shape[0] // 128
    strip = down.shape[0]
    for h in range(per):
        at = h * 2 * units
        lanes = slice(h * 128, (h + 1) * 128)
        gate[lanes, :] = total[at : at + units, :].astype(jnp.float32).T.astype(jnp.bfloat16)
        up[lanes, :] = total[at + units : at + 2 * units, :].astype(jnp.float32).T.astype(jnp.bfloat16)
    base = per * 2 * units
    for j in range(down.shape[1] // 128):
        down[:, j * 128 : (j + 1) * 128] = total[base + j * strip : base + (j + 1) * strip, :]


def shards(tokens, out_grad, expert_ids, route_probs, gate_weight, up_weight, down_weight):
    rows, width = tokens.shape
    half = width // 2
    units = gate_weight.shape[2]
    replicas = lax.axis_size("dp")
    share = width // replicas
    strip = units // replicas
    cut = lax.axis_index("cuts").astype(jnp.int32).reshape(1)
    place = jnp.stack((lax.axis_index("cuts"), lax.axis_index("expert") // 16)).astype(jnp.int32)
    swap = [(0, 1), (1, 0)]
    w_gate, w_up, w_down = gate_weight[:, 0, :], up_weight[:, 0, :], down_weight[:, 0, :]
    bf16 = functools.partial(jax.ShapeDtypeStruct, dtype=jnp.bfloat16)
    ids_t, probs_t = expert_ids.T, route_probs.T

    packed = pl.pallas_call(
        pack_kernel,
        out_shape=bf16((rows, width + 128)),
        in_specs=[SMEM] + [ANY] * 4,
        out_specs=VMEM,
        scratch_shapes=[
            pltpu.VMEM(ids_t.shape, jnp.int32),
            pltpu.VMEM(probs_t.shape, jnp.float32),
            pltpu.SemaphoreType.DMA((3,)),
        ],
        compiler_params=pltpu.CompilerParams(vmem_limit_bytes=60 * 1024 * 1024),
        name="pack",
    )(cut, ids_t, probs_t, tokens, out_grad)
    up_by = [(i, (i + 16) % EXPERTS) for i in range(EXPERTS)]
    down_by = [(j, i) for i, j in up_by]
    behind = lax.ppermute(packed, "expert", up_by)
    ahead = lax.ppermute(packed, "expert", down_by)
    across = lax.ppermute(behind, "expert", up_by)
    sent = pl.pallas_call(
        pick_kernel,
        out_shape=bf16((SLOTS, width)),
        in_specs=[SMEM] + [VMEM] * 4,
        out_specs=VMEM,
        compiler_params=PARAMS,
        name="pick",
    )(place, packed, behind, ahead, across)
    quarters = [[q * 16 + i for i in range(16)] for q in range(4)]
    own = lax.all_to_all(
        sent.reshape(16, 4 * CAP, width), "expert", split_axis=0, concat_axis=0, tiled=True,
        axis_index_groups=quarters,
    ).reshape(SLOTS, width)
    peer = lax.ppermute(own, "cuts", swap)

    flat, backs = pl.pallas_call(
        expert_kernel,
        out_shape=(bf16((replicas, 3 * units * share // 128, 128)), bf16((SLOTS, 2 * units))),
        in_specs=[SMEM] + [VMEM] * 5,
        out_specs=(HBM, VMEM),
        scratch_shapes=[
            pltpu.VMEM((SLOTS, width), jnp.bfloat16),
            pltpu.VMEM((SLOTS, width), jnp.bfloat16),
            pltpu.VMEM((replicas, 3 * units * share // 128, 128), jnp.bfloat16),
            pltpu.SemaphoreType.DMA((replicas,)),
        ],
        compiler_params=pltpu.CompilerParams(vmem_limit_bytes=48 * 1024 * 1024),
        name="expert",
    )(cut, own, peer, w_gate, w_up, w_down)
    total = lax.psum_scatter(flat, "dp", scatter_dimension=0, tiled=True)[0]

    mine, other = pl.pallas_call(
        rows_kernel,
        out_shape=(jax.ShapeDtypeStruct((SLOTS, half), jnp.float32), bf16((SLOTS, half))),
        in_specs=[SMEM] + [VMEM] * 3,
        out_specs=(VMEM, VMEM),
        compiler_params=PARAMS,
        name="rows",
    )(cut, backs, w_gate, w_up)
    mine = mine + lax.ppermute(other, "cuts", swap).astype(jnp.float32)
    returned = lax.all_to_all(
        mine.astype(jnp.bfloat16).reshape(16, 4, CAP, half).transpose(1, 0, 2, 3)
        .reshape(EXPERTS, CAP, half),
        "expert", split_axis=0, concat_axis=0, tiled=True,
    ).reshape(SLOTS, half)
    result = pl.pallas_call(
        combine_kernel,
        out_shape=bf16((rows, half)),
        in_specs=[VMEM] * 2,
        out_specs=VMEM,
        compiler_params=PARAMS,
        name="combine",
    )(ids_t, returned)

    gate_grad, up_grad, down_grad = pl.pallas_call(
        unpack_kernel,
        out_shape=(bf16((share, units)), bf16((share, units)), bf16((strip, width))),
        in_specs=[VMEM],
        out_specs=(VMEM,) * 3,
        compiler_params=PARAMS,
        name="unpack",
    )(total)
    return (result, gate_grad[:, None, :], up_grad[:, None, :], down_grad[:, None, :])


def solution(mesh):
    placed = (
        P(("expert", "dp"), None),
        P(("expert", "dp"), None),
        P(("expert", "dp"), None),
        P(("expert", "dp"), None),
        P(None, "expert", "cuts"),
        P(None, "expert", "cuts"),
        P("cuts", "expert", None),
    )
    return jax.shard_map(
        shards,
        mesh=mesh,
        in_specs=placed,
        out_specs=(
            P(("expert", "dp"), "cuts"),
            P("dp", "expert", "cuts"),
            P("dp", "expert", "cuts"),
            P(("cuts", "dp"), "expert", None),
        ),
        check_vma=False,
    )
```

```python
import functools

import jax
import jax.numpy as jnp
from jax import lax
from jax.experimental import pallas as pl
from jax.experimental.pallas import tpu as pltpu
from jax.sharding import PartitionSpec as P

EXPERTS = 64
CAP = 4
SLOTS = EXPERTS * CAP
VMEM = pl.BlockSpec(memory_space=pltpu.VMEM)
SMEM = pl.BlockSpec(memory_space=pltpu.SMEM)
ANY = pl.BlockSpec(memory_space=pl.ANY)
HBM = pl.BlockSpec(memory_space=pltpu.HBM)
PARAMS = pltpu.CompilerParams(vmem_limit_bytes=32 * 1024 * 1024)


def dot(a, b, da, db, precision=None):
    return lax.dot_general(
        a, b, (((da,), (db,)), ((), ())), precision=precision, preferred_element_type=jnp.float32
    )


def pack_kernel(cut, ids_hbm, probs_hbm, tokens, grads, packed, ids_t, probs_t, sems):
    top = ids_t.shape[0]
    width = tokens.shape[1]
    body = packed.at[:, pl.ds(0, width)]
    load_ids = pltpu.make_async_copy(ids_hbm, ids_t, sems.at[0])
    load_probs = pltpu.make_async_copy(probs_hbm, probs_t, sems.at[1])
    load_ids.start()
    load_probs.start()

    @pl.when(cut[0] == 0)
    def _():
        pltpu.make_async_copy(tokens, body, sems.at[2]).start()

    @pl.when(cut[0] != 0)
    def _():
        pltpu.make_async_copy(grads, body, sems.at[2]).start()

    load_ids.wait()
    load_probs.wait()
    probs = probs_t[...]
    high = probs.astype(jnp.bfloat16).astype(jnp.float32)
    middle = (probs - high).astype(jnp.bfloat16).astype(jnp.float32)
    low = probs - high - middle
    terms = jnp.concatenate((ids_t[...].astype(jnp.float32), high, middle, low), axis=0)
    row = lax.broadcasted_iota(jnp.int32, (4 * top, 128), 0)
    unit = jnp.where(row == lax.broadcasted_iota(jnp.int32, (4 * top, 128), 1), 1.0, 0.0)
    packed[:, width:] = dot(
        terms.astype(jnp.bfloat16), unit.astype(jnp.bfloat16), 0, 0
    ).astype(jnp.bfloat16)
    pltpu.make_async_copy(tokens, body, sems.at[2]).wait()


def ranks(names):
    rows = names.shape[0]
    before = lax.broadcasted_iota(jnp.int32, (rows, rows), 0) > lax.broadcasted_iota(
        jnp.int32, (rows, rows), 1
    )
    return dot(jnp.where(before, 1.0, 0.0).astype(jnp.bfloat16), names.astype(jnp.bfloat16), 1, 0)


def pick_kernel(place, own, behind, ahead, across, sent):
    rows, packed = own.shape
    width = sent.shape[1]
    f32 = jnp.float32
    blocks = (own, behind, ahead, across)
    source = jnp.concatenate([b[:, :width].astype(f32) for b in blocks], axis=0).astype(jnp.bfloat16)
    facts = jnp.concatenate([b[:, width:].astype(f32) for b in blocks], axis=0)
    total = 4 * rows
    group = place[1]
    token = lax.broadcasted_iota(jnp.int32, (total, SLOTS), 0)
    lane = lax.broadcasted_iota(jnp.int32, (total, SLOTS), 1)
    shift = jnp.where(
        token < rows, 0, jnp.where(token < 2 * rows, 3, jnp.where(token < 3 * rows, 1, 2))
    )
    block = jnp.bitwise_and(group + shift, 3)
    here = block == jnp.bitwise_and(lax.shift_right_logical(lane, 2), 3)
    expert = (group * 16 + lax.shift_right_logical(lane, 4)).astype(f32)
    names = jnp.zeros((total, SLOTS), f32)
    weight = jnp.zeros((total, SLOTS), f32)
    top = 8
    prob = facts[:, top : 2 * top] + facts[:, 2 * top : 3 * top] + facts[:, 3 * top : 4 * top]
    for k in range(top):
        same = jnp.logical_and(facts[:, k : k + 1] == expert, here)
        names = names + jnp.where(same, 1.0, 0.0)
        weight = weight + jnp.where(same, prob[:, k : k + 1], 0.0)
    slot = jnp.bitwise_and(lane, CAP - 1).astype(f32)
    hit = jnp.where(ranks(names) == slot, names, 0.0)

    @pl.when(place[0] == 0)
    def _():
        sent[...] = dot(hit.astype(jnp.bfloat16), source, 0, 0).astype(jnp.bfloat16)

    @pl.when(place[0] != 0)
    def _():
        factor = hit * weight
        high = factor.astype(jnp.bfloat16)
        middle = (factor - high.astype(f32)).astype(jnp.bfloat16)
        low = (factor - high.astype(f32) - middle.astype(f32)).astype(jnp.bfloat16)
        sent[...] = (
            dot(high, source, 0, 0) + (dot(middle, source, 0, 0) + dot(low, source, 0, 0))
        ).astype(jnp.bfloat16)


def combine_kernel(ids_t, returned, out):
    top, rows = ids_t.shape
    unit = jnp.where(
        lax.broadcasted_iota(jnp.int32, (top, top), 0) == lax.broadcasted_iota(jnp.int32, (top, top), 1),
        1.0, 0.0,
    )
    ids = dot(ids_t[...].astype(jnp.bfloat16), unit.astype(jnp.bfloat16), 0, 0)
    lane = lax.broadcasted_iota(jnp.int32, (rows, SLOTS), 1)
    expert = lax.shift_right_logical(lane, 2).astype(jnp.float32)
    names = jnp.zeros((rows, SLOTS), jnp.float32)
    for k in range(top):
        names = names + jnp.where(ids[:, k : k + 1] == expert, 1.0, 0.0)
    slot = jnp.bitwise_and(lane, CAP - 1).astype(jnp.float32)
    hit = jnp.where(ranks(names) == slot, names, 0.0)
    out[...] = dot(hit.astype(jnp.bfloat16), returned[...], 1, 0).astype(jnp.bfloat16)


def expert_kernel(
    place, own, peer, gate, up, down_hbm, flat_hbm, backs, rows, grads, down, flat, down_sem, out_sems
):
    load_down = pltpu.make_async_copy(down_hbm, down, down_sem)
    load_down.start()

    @pl.when(place[0] == 0)
    def _():
        rows[...] = own[...]
        grads[...] = peer[...]

    @pl.when(place[0] != 0)
    def _():
        rows[...] = peer[...]
        grads[...] = own[...]

    gate_val = dot(rows[...], gate[...], 1, 0)
    up_val = dot(rows[...], up[...], 1, 0)
    sigma = 1.0 / (1.0 + jnp.exp(-gate_val))
    activated = gate_val * sigma
    slope = sigma * (1.0 + gate_val * (1.0 - sigma))
    hidden_t = (activated * up_val).T.astype(jnp.bfloat16)
    width = rows.shape[1]
    units = gate.shape[1]
    replicas = flat.shape[0]
    strip = units // replicas
    share = width // replicas
    per = share // 128
    for i in range(replicas):
        columns = slice(i * share, (i + 1) * share)
        part = dot(hidden_t, grads[:, columns], 1, 0).astype(jnp.bfloat16)
        for h in range(per):
            lanes = slice(h * 128, (h + 1) * 128)
            start = 2 * per * units + (i * per + h) * strip
            for j in range(replicas):
                flat[j, start : start + strip, :] = part[j * strip : (j + 1) * strip, lanes]
    load_down.wait()
    back_hid = dot(grads[...], down[...], 1, 1)
    both = jnp.concatenate((back_hid * up_val * slope, back_hid * activated), axis=1)
    backs[...] = both.astype(jnp.bfloat16)
    both_t = both.T.astype(jnp.bfloat16)
    outs = [
        pltpu.make_async_copy(flat.at[i], flat_hbm.at[i], out_sems.at[i]) for i in range(replicas)
    ]
    for i in range(replicas):
        columns = slice(i * share, (i + 1) * share)
        part = dot(both_t, rows[:, columns], 1, 0).astype(jnp.bfloat16)
        for h in range(per):
            flat[i, h * 2 * units : (h + 1) * 2 * units, :] = part[:, h * 128 : (h + 1) * 128]
        outs[i].start()
    for copy in outs:
        copy.wait()


def rows_kernel(cut, backs, gate, up, mine, other):
    half = mine.shape[1]
    units = gate.shape[1]

    def part(c):
        at = pl.ds(pl.multiple_of(c * half, half), half)
        return dot(backs[:, :units], gate[at, :], 1, 1) + dot(backs[:, units:], up[at, :], 1, 1)

    other[...] = part(1 - cut[0]).astype(jnp.bfloat16)
    mine[...] = part(cut[0])


def unpack_kernel(total, gate, up, down):
    units = gate.shape[1]
    per = gate.shape[0] // 128
    strip = down.shape[0]
    for h in range(per):
        at = h * 2 * units
        lanes = slice(h * 128, (h + 1) * 128)
        gate[lanes, :] = total[at : at + units, :].astype(jnp.float32).T.astype(jnp.bfloat16)
        up[lanes, :] = total[at + units : at + 2 * units, :].astype(jnp.float32).T.astype(jnp.bfloat16)
    base = per * 2 * units
    for j in range(down.shape[1] // 128):
        down[:, j * 128 : (j + 1) * 128] = total[base + j * strip : base + (j + 1) * strip, :]


def shards(tokens, out_grad, expert_ids, route_probs, gate_weight, up_weight, down_weight):
    rows, width = tokens.shape
    half = width // 2
    units = gate_weight.shape[2]
    replicas = lax.axis_size("dp")
    share = width // replicas
    strip = units // replicas
    cut = lax.axis_index("cuts").astype(jnp.int32).reshape(1)
    place = jnp.stack((lax.axis_index("cuts"), lax.axis_index("expert") // 16)).astype(jnp.int32)
    swap = [(0, 1), (1, 0)]
    w_gate, w_up, w_down = gate_weight[:, 0, :], up_weight[:, 0, :], down_weight[:, 0, :]
    bf16 = functools.partial(jax.ShapeDtypeStruct, dtype=jnp.bfloat16)
    ids_t, probs_t = expert_ids.T, route_probs.T

    packed = pl.pallas_call(
        pack_kernel,
        out_shape=bf16((rows, width + 128)),
        in_specs=[SMEM] + [ANY] * 4,
        out_specs=VMEM,
        scratch_shapes=[
            pltpu.VMEM(ids_t.shape, jnp.int32),
            pltpu.VMEM(probs_t.shape, jnp.float32),
            pltpu.SemaphoreType.DMA((3,)),
        ],
        compiler_params=pltpu.CompilerParams(vmem_limit_bytes=60 * 1024 * 1024),
        name="pack",
    )(cut, ids_t, probs_t, tokens, out_grad)
    up_by = [(i, (i + 16) % EXPERTS) for i in range(EXPERTS)]
    down_by = [(j, i) for i, j in up_by]
    behind = lax.ppermute(packed, "expert", up_by)
    ahead = lax.ppermute(packed, "expert", down_by)
    across = lax.ppermute(behind, "expert", up_by)
    sent = pl.pallas_call(
        pick_kernel,
        out_shape=bf16((SLOTS, width)),
        in_specs=[SMEM] + [VMEM] * 4,
        out_specs=VMEM,
        compiler_params=PARAMS,
        name="pick",
    )(place, packed, behind, ahead, across)
    quarters = [[q * 16 + i for i in range(16)] for q in range(4)]
    own = lax.all_to_all(
        sent.reshape(16, 4 * CAP, width), "expert", split_axis=0, concat_axis=0, tiled=True,
        axis_index_groups=quarters,
    ).reshape(SLOTS, width)
    peer = lax.ppermute(own, "cuts", swap)

    flat, backs = pl.pallas_call(
        expert_kernel,
        out_shape=(bf16((replicas, 3 * units * share // 128, 128)), bf16((SLOTS, 2 * units))),
        in_specs=[SMEM] + [VMEM] * 4 + [ANY],
        out_specs=(HBM, VMEM),
        scratch_shapes=[
            pltpu.VMEM((SLOTS, width), jnp.bfloat16),
            pltpu.VMEM((SLOTS, width), jnp.bfloat16),
            pltpu.VMEM((units, width), jnp.bfloat16),
            pltpu.VMEM((replicas, 3 * units * share // 128, 128), jnp.bfloat16),
            pltpu.SemaphoreType.DMA,
            pltpu.SemaphoreType.DMA((replicas,)),
        ],
        compiler_params=pltpu.CompilerParams(vmem_limit_bytes=48 * 1024 * 1024),
        name="expert",
    )(cut, own, peer, w_gate, w_up, w_down)
    total = lax.psum_scatter(flat, "dp", scatter_dimension=0, tiled=True)[0]

    mine, other = pl.pallas_call(
        rows_kernel,
        out_shape=(jax.ShapeDtypeStruct((SLOTS, half), jnp.float32), bf16((SLOTS, half))),
        in_specs=[SMEM] + [VMEM] * 3,
        out_specs=(VMEM, VMEM),
        compiler_params=PARAMS,
        name="rows",
    )(cut, backs, w_gate, w_up)
    mine = mine + lax.ppermute(other, "cuts", swap).astype(jnp.float32)
    returned = lax.all_to_all(
        mine.astype(jnp.bfloat16).reshape(16, 4, CAP, half).transpose(1, 0, 2, 3)
        .reshape(EXPERTS, CAP, half),
        "expert", split_axis=0, concat_axis=0, tiled=True,
    ).reshape(SLOTS, half)
    result = pl.pallas_call(
        combine_kernel,
        out_shape=bf16((rows, half)),
        in_specs=[VMEM] * 2,
        out_specs=VMEM,
        compiler_params=PARAMS,
        name="combine",
    )(ids_t, returned)

    gate_grad, up_grad, down_grad = pl.pallas_call(
        unpack_kernel,
        out_shape=(bf16((share, units)), bf16((share, units)), bf16((strip, width))),
        in_specs=[VMEM],
        out_specs=(VMEM,) * 3,
        compiler_params=pltpu.CompilerParams(vmem_limit_bytes=60 * 1024 * 1024),
        name="unpack",
    )(total)
    return (result, gate_grad[:, None, :], up_grad[:, None, :], down_grad[:, None, :])


def solution(mesh):
    placed = (
        P(("expert", "dp"), None),
        P(("expert", "dp"), None),
        P(("expert", "dp"), None),
        P(("expert", "dp"), None),
        P(None, "expert", "cuts"),
        P(None, "expert", "cuts"),
        P("cuts", "expert", None),
    )
    return jax.shard_map(
        shards,
        mesh=mesh,
        in_specs=placed,
        out_specs=(
            P(("expert", "dp"), "cuts"),
            P("dp", "expert", "cuts"),
            P("dp", "expert", "cuts"),
            P(("cuts", "dp"), "expert", None),
        ),
        check_vma=False,
    )
```
